32 devices in a mesh: lag: 16 (over z, y, x), col: 2 (over core).
Axes of the slice: x: 2, y: 2, z: 4, core: 2. Of those that a mesh axis runs over, the one named last changes fastest.
Arguments:
- tap_matrices: bfloat16 [16, 1024, 2048], P('lag', None, 'col'), may hold values from -0.125 to 0.125
- density_history: bfloat16 [64, 2048, 128], P('lag', 'col'), may hold values from -6 to 6
- offsets: int32 [16], P('lag'), may hold values from 0 to 3
- column_slots: int32 [2, 128], P('col'), may hold values from 0 to 127, each once within a row
Outputs:
- history_sum: float32 [16, 1024, 3, 128], P('lag', 'col')
The draws below stay inside these ranges and needn't reach their ends.
Inputs may be any that keep to these rules, and one draw needn't show every extreme that they name: Section s reads history slots s * 4 + offsets[s] to s * 4 + offsets[s] + 2. `column_slots`: each row is a permutation of the 128 stored columns.
All inputs are finite; a program needn't handle non-finite values.
Results may differ from the reference program's by a relative error of at most 0.0003.
Values may be sent and summed in bfloat16 or wider, within the bound.
No kernel may reach another device: no remote copies, remote signals or barrier semaphores. Data moves between devices by JAX's collectives and lax.ppermute only.
A program may use at most 128 MiB of HBM per device.

```python
import jax
import jax.numpy as jnp
from jax import lax

M = 1024
C = 1024
E = 128
SLOTS = 4
TICKS = 3
SECTIONS = 16
COLS = 2
SRC = 2048
HSLOTS = 64
N_COL = 2


def set_ends(drawn, key, smallest, high):
    longest = drawn.shape.index(max(drawn.shape))
    spots = []
    for shift in (0, 1):
        where = [jax.random.randint(jax.random.fold_in(key, axis), (), 0, length) for axis, length in enumerate(drawn.shape)]
        where[longest] = (where[longest] + shift) % drawn.shape[longest]
        spots.append(tuple(where))
    return drawn.at[spots[0]].set(smallest).at[spots[1]].set(high)


def block_scale(key, dims, cuts, smallest, high):
    factor_of, own = 1.0, jax.random.fold_in(key, 6)
    for position, blocks in cuts:
        heights = jnp.exp(jax.random.uniform(jax.random.fold_in(own, position), (blocks,), jnp.float32, smallest / len(cuts), high / len(cuts)))
        factor_of = factor_of * jnp.repeat(heights, dims[position] // blocks).reshape([-1 if axis == position else 1 for axis in range(len(dims))])
    return factor_of


def scatter_about(own_key, dims, width, bound, cuts=(), kind=jnp.bfloat16):
    entries = width * jax.random.normal(own_key, dims, jnp.float32)
    if cuts:
        entries = entries * block_scale(own_key, dims, cuts, -0.22, 0.18)
    return jnp.clip(entries, -bound, bound).astype(kind)


def setup_inputs(seed: int = 0) -> dict:
    keys = jax.random.split(jax.random.key(seed), 5)
    tap_matrices = scatter_about(keys[0], (SECTIONS, M, SRC), SRC ** -0.5, 0.125, ((0, 16), (2, 2)))
    density_history = scatter_about(keys[1], (HSLOTS, SRC, E), 1.0, 6.0, ((0, 16), (1, 2)))
    offsets = set_ends(jax.random.randint(keys[2], (SECTIONS,), 0, SLOTS), jax.random.fold_in(keys[2], 1), 0, SLOTS - 1).astype(jnp.int32)
    column_slots = jax.vmap(lambda own: jax.random.permutation(own, E))(jax.random.split(keys[3], COLS)).reshape((COLS, E)).astype(jnp.int32)
    return dict(tap_matrices=tap_matrices, density_history=density_history, offsets=offsets, column_slots=column_slots)


def reorder_group(group_data, group_slots):
    return jnp.take(group_data, group_slots, axis=2)


def reference(tap_matrices, density_history, offsets, column_slots):
    slots_all = density_history.shape[0]
    grouped = density_history.reshape(slots_all, N_COL, C, E)
    ordered = jax.vmap(reorder_group, in_axes=(1, 0), out_axes=1)(grouped, column_slots)
    padded = jnp.concatenate([ordered, jnp.zeros((SLOTS, N_COL, C, E), jnp.bfloat16)], axis=0)

    def advance(running, inputs):
        tap_matrix, offset, section = inputs
        first_slot = (section * SLOTS + offset).astype(jnp.int32)
        densities = lax.dynamic_slice_in_dim(padded, first_slot, TICKS, 0)
        tap_blocks = tap_matrix.reshape(M, N_COL, C)
        partials = jnp.einsum("mgc,tgce->gmte", tap_blocks.astype(jnp.float32), densities.astype(jnp.float32))
        section_sum = jnp.sum(partials, axis=0)
        running = running + section_sum
        return running, running

    start_sum = jnp.zeros((M, TICKS, E), jnp.float32)
    sections_idx = jnp.arange(SECTIONS, dtype=jnp.int32)
    _, history_sum = lax.scan(advance, start_sum, (tap_matrices, offsets, sections_idx))
    return history_sum
```

```python
import functools

import jax
import jax.numpy as jnp
from jax import lax
from jax.experimental import pallas as pl
from jax.experimental.pallas import tpu as pltpu
from jax.sharding import PartitionSpec as P

TICKS = 3
INNER = 4
VMEM = pl.BlockSpec(memory_space=pltpu.VMEM)
SMEM = pl.BlockSpec(memory_space=pltpu.SMEM)
LIMIT = pltpu.CompilerParams(vmem_limit_bytes=40 * 2**20)


def call(kernel, out_shape, ins, scratch=()):
    return pl.pallas_call(
        kernel,
        out_shape=out_shape,
        in_specs=[SMEM if a.ndim == 1 else VMEM for a in ins],
        out_specs=jax.tree.map(lambda _: VMEM, out_shape),
        scratch_shapes=list(scratch),
        compiler_params=LIMIT,
    )(*ins)


def swapped(value, axis, mask):
    count = lax.axis_size(axis)
    return lax.ppermute(value, axis, [(i, i ^ mask) for i in range(count)])


def pack(x, ref):
    half = x.shape[1] // 2
    high = jnp.maximum(jnp.max(jnp.abs(x), axis=1, keepdims=True), 2.0**-100)
    power = jnp.floor(jnp.log2(high)) + 1.0
    q = jnp.clip(jnp.round(x * jnp.exp2(15.0 - power)), -32768.0, 32767.0).astype(jnp.int32)
    words = (q[:, :half] & 0xFFFF) | (q[:, half:] << 16)
    for t in range(TICKS):
        ref[t * half : (t + 1) * half, :] = words[t]
    scales = power.astype(jnp.int32)
    tail = jnp.concatenate([scales[t] for t in range(TICKS)] + [jnp.zeros((8 - TICKS, x.shape[2]), jnp.int32)], axis=0)
    ref[TICKS * half : TICKS * half + 8, :] = tail


def unpack(ref, half):
    tail = ref[TICKS * half : TICKS * half + 8, :].astype(jnp.float32)
    unit = jnp.exp2(tail - 15.0)
    ticks = []
    for t in range(TICKS):
        words = ref[t * half : (t + 1) * half, :]
        both = jnp.concatenate([(words << 16) >> 16, words >> 16], axis=0)
        ticks.append(both.astype(jnp.float32) * unit[t : t + 1])
    return jnp.stack(ticks)


def product_kernel(n_col, where, offset, taps, own, newer, slots, keep, *rest):
    sends, window = rest[:-1], rest[-1]
    slots_own, source, width = own.shape
    rows = keep.shape[1]
    place, last = where[0], where[1]
    chosen = lax.broadcasted_iota(jnp.int32, (width, width), 0) == slots[...]
    chosen = chosen.astype(jnp.float32).astype(jnp.bfloat16)
    for t in range(TICKS):
        slot = offset[0] + t
        lanes = slice(t * width, (t + 1) * width)

        @pl.when(slot < slots_own)
        def _():
            part = jnp.dot(own[jnp.minimum(slot, slots_own - 1)], chosen, preferred_element_type=jnp.float32)
            window[:, lanes] = part.astype(jnp.bfloat16)

        @pl.when(slot >= slots_own)
        def _():
            part = jnp.dot(newer[jnp.maximum(slot - slots_own, 0)], chosen, preferred_element_type=jnp.float32)
            window[:, lanes] = jnp.where(last == 1, 0.0, part).astype(jnp.bfloat16)

    step = min(rows, 256)
    for k, out in enumerate((keep, *sends)):
        for start in range(0, rows, step):
            first = pl.multiple_of((place ^ k) * rows + start, step)
            result = jnp.dot(taps[pl.ds(first, step), :], window[...], preferred_element_type=jnp.float32)
            for t in range(TICKS):
                out[t, start : start + step, :] = result[:, t * width : (t + 1) * width]


def split_kernel(n_col, where, *refs):
    parts, (own, mine, *sends) = refs[:n_col], refs[n_col:]
    total = parts[0][...]
    for part in parts[1:]:
        total = total + part[...]
    own[...] = total
    piece = own.shape[1] // INNER
    for k, out in enumerate((mine, *sends)):
        first = pl.multiple_of((where[2] ^ k) * piece, piece)
        value = own[:, pl.ds(first, piece), :]
        if k:
            pack(value, out)
        else:
            out[...] = value


def total_kernel(mine, *refs):
    received, out = refs[:-1], refs[-1]
    half = mine.shape[1] // 2
    total = mine[...]
    for ref in received:
        total = total + unpack(ref, half)
    pack(total, out)


def prefix_kernel(n_outer, where, mine, *refs):
    received, totals, (base, *sends) = refs[: INNER - 1], refs[INNER - 1 : INNER + n_outer - 2], refs[INNER + n_outer - 2 :]
    half = mine.shape[1] // 2
    place, group = where[2], where[3]
    earlier = jnp.zeros(mine.shape, jnp.float32)
    for k, ref in enumerate(totals, 1):
        earlier = earlier + jnp.where((group ^ k) < group, unpack(ref, half), 0.0)
    terms = [mine[...]] + [unpack(ref, half) for ref in received]
    for k, out in enumerate((base, *sends)):
        value = earlier
        for m, term in enumerate(terms):
            if m != k:
                value = value + jnp.where((place ^ m) < (place ^ k), term, 0.0)
        if k:
            pack(value, out)
        else:
            out[...] = value


def finish_kernel(where, own, base, *refs):
    received, out = refs[:-1], refs[-1]
    piece = base.shape[1]
    for k, ref in enumerate((base, *received)):
        first = pl.multiple_of((where[2] ^ k) * piece, piece)
        older = unpack(ref, piece // 2) if k else ref[...]
        out[:, pl.ds(first, piece), :] = own[:, pl.ds(first, piece), :] + older


def local(tap_matrices, density_history, offsets, column_slots):
    n_lag, n_col = lax.axis_size("lag"), lax.axis_size("col")
    n_outer = n_lag // INNER
    lag, col = lax.axis_index("lag"), lax.axis_index("col")
    where = jnp.stack([col, (lag == n_lag - 1).astype(jnp.int32), lag % INNER, lag // INNER]).astype(jnp.int32)
    taps = tap_matrices[0]
    unknowns, source = taps.shape
    width = column_slots.shape[1]
    rows = unknowns // n_col
    piece = rows // INNER
    f32 = functools.partial(jax.ShapeDtypeStruct, dtype=jnp.float32)
    packed = jax.ShapeDtypeStruct((TICKS * piece // 2 + 8, width), jnp.int32)

    newer = lax.ppermute(density_history[: TICKS - 1], "lag", [(i, (i - 1) % n_lag) for i in range(n_lag)])
    products = call(
        functools.partial(product_kernel, n_col),
        [f32((TICKS, rows, width))] * n_col,
        [where, offsets, taps, density_history, newer, column_slots],
        [pltpu.VMEM((source, TICKS * width), jnp.bfloat16)],
    )
    others = [swapped(value, "col", k) for k, value in enumerate(products[1:], 1)]
    own, mine, *sends = call(
        functools.partial(split_kernel, n_col),
        [f32((TICKS, rows, width)), f32((TICKS, piece, width))] + [packed] * (INNER - 1),
        [where, products[0], *others],
    )
    received = [swapped(value, "lag", k) for k, value in enumerate(sends, 1)]
    [total] = call(total_kernel, [packed], [mine, *received])
    totals = [swapped(total, "lag", k * INNER) for k in range(1, n_outer)]
    base, *sends = call(
        functools.partial(prefix_kernel, n_outer),
        [f32((TICKS, piece, width))] + [packed] * (INNER - 1),
        [where, mine, *received, *totals],
    )
    received = [swapped(value, "lag", k) for k, value in enumerate(sends, 1)]
    [history_sum] = call(finish_kernel, [f32((TICKS, rows, width))], [where, own, base, *received])
    return jnp.transpose(history_sum, (1, 0, 2))[None]


def solution(mesh):
    return jax.shard_map(
        local,
        mesh=mesh,
        in_specs=(P("lag", None, "col"), P("lag", "col", None), P("lag"), P("col", None)),
        out_specs=P("lag", "col", None, None),
        check_vma=False,
    )
```

```python
import functools

import jax
import jax.numpy as jnp
from jax import lax
from jax.experimental import pallas as pl
from jax.experimental.pallas import tpu as pltpu
from jax.sharding import PartitionSpec as P

TICKS = 3
PARTS = 2
INNER = 4
VMEM = pl.BlockSpec(memory_space=pltpu.VMEM)
SMEM = pl.BlockSpec(memory_space=pltpu.SMEM)
HBM = pl.BlockSpec(memory_space=pl.ANY)
LIMIT = pltpu.CompilerParams(vmem_limit_bytes=40 * 2**20)
FULL = pltpu.CompilerParams(vmem_limit_bytes=60 * 2**20)


def call(kernel, out_shape, ins, scratch=(), outs=VMEM, params=LIMIT):
    return pl.pallas_call(
        kernel,
        out_shape=out_shape,
        in_specs=[SMEM if a.ndim == 1 else VMEM for a in ins],
        out_specs=jax.tree.map(lambda _: outs, out_shape),
        scratch_shapes=list(scratch),
        compiler_params=params,
    )(*ins)


def swapped(value, axis, mask):
    count = lax.axis_size(axis)
    return lax.ppermute(value, axis, [(i, i ^ mask) for i in range(count)])


def pack(x, ref):
    ticks, half = x.shape[0], x.shape[1] // 2
    high = jnp.maximum(jnp.max(jnp.abs(x), axis=1, keepdims=True), 2.0**-100)
    power = jnp.floor(jnp.log2(high)) + 1.0
    q = jnp.clip(jnp.round(x * jnp.exp2(15.0 - power)), -32768.0, 32767.0).astype(jnp.int32)
    words = (q[:, :half] & 0xFFFF) | (q[:, half:] << 16)
    for t in range(ticks):
        ref[t * half : (t + 1) * half, :] = words[t]
    scales = power.astype(jnp.int32)
    tail = jnp.concatenate([scales[t] for t in range(ticks)] + [jnp.zeros((8 - ticks, x.shape[2]), jnp.int32)], axis=0)
    ref[ticks * half : ticks * half + 8, :] = tail


def unpack(ref, half):
    ticks = (ref.shape[0] - 8) // half
    unit = jnp.exp2(ref[ticks * half : ticks * half + 8, :].astype(jnp.float32) - 15.0)
    values = []
    for t in range(ticks):
        words = ref[t * half : (t + 1) * half, :]
        both = jnp.concatenate([(words << 16) >> 16, words >> 16], axis=0)
        values.append(both.astype(jnp.float32) * unit[t : t + 1])
    return jnp.stack(values)


def chooser(slots):
    width = slots.shape[1]
    hit = lax.broadcasted_iota(jnp.int32, (width, width), 0) == slots[...]
    return hit.astype(jnp.float32).astype(jnp.bfloat16)


def prepare_kernel(where, offset, taps, own, slots, window, *sends):
    slots_own, _, width = own.shape
    chosen = chooser(slots)
    for t in range(TICKS):
        slot = offset[0] + t
        part = jnp.dot(own[jnp.minimum(slot, slots_own - 1)], chosen, preferred_element_type=jnp.float32)
        window[:, t * width : (t + 1) * width] = jnp.where(slot < slots_own, part, 0.0).astype(jnp.bfloat16)
    for k, out in enumerate(sends, 1):
        rows = out.shape[0]
        first = (where[0] ^ (1 + (k - 1) // PARTS)) * rows * PARTS + ((k - 1) % PARTS) * rows
        out[...] = taps[pl.ds(pl.multiple_of(first, rows), rows), :]


def base_kernel(n_col, where, taps, *refs):
    others, windows, out = refs[: (n_col - 1) * PARTS], refs[(n_col - 1) * PARTS : -1], refs[-1]
    rows, width = out.shape[1], out.shape[2]
    mine = taps[pl.ds(pl.multiple_of(where[0] * rows, rows), rows), :]
    total = jnp.dot(mine, windows[0][...], preferred_element_type=jnp.float32)
    for i, window in enumerate(windows[1:]):
        other = jnp.concatenate([ref[...] for ref in others[i * PARTS : (i + 1) * PARTS]], axis=0)
        total = total + jnp.dot(other, window[...], preferred_element_type=jnp.float32)
    for t in range(TICKS):
        out[t] = total[:, t * width : (t + 1) * width]


def late_kernel(n_col, where, offset, taps, base, *refs):
    cut = (n_col - 1) * PARTS
    others, newer, slots = refs[:cut], refs[cut : cut + n_col], refs[cut + n_col : cut + 2 * n_col]
    own, mine, *sends = refs[cut + 2 * n_col :]
    _, rows, width = base.shape
    local = taps[pl.ds(pl.multiple_of(where[0] * rows, rows), rows), :]
    total = 0.0
    for i in range(n_col):
        chosen = chooser(slots[i])
        parts = [jnp.dot(newer[i][j], chosen, preferred_element_type=jnp.float32) for j in range(TICKS - 1)]
        rhs = jnp.concatenate([part.astype(jnp.bfloat16) for part in parts], axis=1)
        lhs = jnp.concatenate([ref[...] for ref in others[(i - 1) * PARTS : i * PARTS]], axis=0) if i else local
        total = total + jnp.dot(lhs, rhs, preferred_element_type=jnp.float32)
    for t in range(TICKS):
        value = base[t]
        for j in range(t):
            used = (offset[0] + t == where[1] + j) & (where[2] == 0)
            value = value + jnp.where(used, total[:, j * width : (j + 1) * width], 0.0)
        own[t] = value
    piece = rows // INNER
    for k, out in enumerate((mine, *sends)):
        first = pl.multiple_of((where[3] ^ k) * piece, piece)
        value = own[:, pl.ds(first, piece), :]
        if k:
            pack(value, out)
        else:
            out[...] = value


def total_kernel(mine, *refs):
    received, out = refs[:-1], refs[-1]
    half = mine.shape[1] // 2
    total = mine[...]
    for ref in received:
        total = total + unpack(ref, half)
    pack(total, out)


def prefix_kernel(n_outer, where, mine, *refs):
    received, totals, (base, *sends) = refs[: INNER - 1], refs[INNER - 1 : INNER + n_outer - 2], refs[INNER + n_outer - 2 :]
    half = mine.shape[1] // 2
    place, group = where[3], where[4]
    earlier = jnp.zeros(mine.shape, jnp.float32)
    for k, ref in enumerate(totals, 1):
        earlier = earlier + jnp.where((group ^ k) < group, unpack(ref, half), 0.0)
    terms = [mine[...]] + [unpack(ref, half) for ref in received]
    for k, out in enumerate((base, *sends)):
        value = earlier
        for m, term in enumerate(terms):
            if m != k:
                value = value + jnp.where((place ^ m) < (place ^ k), term, 0.0)
        if k:
            pack(value, out)
        else:
            out[...] = value


def finish_kernel(where, own, base, *refs):
    received, (out, ready, sems) = refs[:-3], refs[-3:]
    piece = base.shape[1]
    copies = []
    for k, ref in enumerate((base, *received)):
        first = pl.multiple_of((where[3] ^ k) * piece, piece)
        older = unpack(ref, piece // 2) if k else ref[...]
        ready[k] = own[:, pl.ds(first, piece), :] + older
        copies.append(pltpu.make_async_copy(ready.at[k], out.at[:, pl.ds(first, piece), :], sems.at[k]))
        copies[-1].start()
    for copy in copies:
        copy.wait()


def among_members(values):
    order = range(len(values), 0, -1)
    arrived = {k: swapped(values[k - 1], "lag", k) for k in order}
    return [arrived[k] for k in range(1, len(values) + 1)]


def local(tap_matrices, density_history, offsets, column_slots):
    n_lag, n_col = lax.axis_size("lag"), lax.axis_size("col")
    n_outer = n_lag // INNER
    lag, col = lax.axis_index("lag"), lax.axis_index("col")
    slots_own, source, width = density_history.shape
    last = (lag == n_lag - 1).astype(jnp.int32)
    where = jnp.stack([col, jnp.int32(slots_own), last, lag & (INNER - 1), lag // INNER]).astype(jnp.int32)
    taps = tap_matrices[0]
    rows = taps.shape[0] // n_col
    piece = rows // INNER

    def f32(height):
        return jax.ShapeDtypeStruct((TICKS, height, width), jnp.float32)

    def bf16(*shape):
        return jax.ShapeDtypeStruct(shape, jnp.bfloat16)

    packed = jax.ShapeDtypeStruct((TICKS * piece // 2 + 8, width), jnp.int32)

    newer = lax.ppermute(density_history[: TICKS - 1], "lag", [(i, (i - 1) % n_lag) for i in range(n_lag)])
    window, *tap_sends = call(
        prepare_kernel,
        [bf16(source, TICKS * width)] + [bf16(rows // PARTS, source)] * ((n_col - 1) * PARTS),
        [where, offsets, taps, density_history, column_slots],
    )
    others = [swapped(value, "col", 1 + i // PARTS) for i, value in enumerate(tap_sends)]
    windows = [window] + [swapped(window, "col", k) for k in range(1, n_col)]
    [base] = call(functools.partial(base_kernel, n_col), [f32(rows)], [where, taps, *others, *windows])
    newer = [newer] + [swapped(newer, "col", k) for k in range(1, n_col)]
    slots = [column_slots] + [swapped(column_slots, "col", k) for k in range(1, n_col)]
    own, mine, *sends = call(
        functools.partial(late_kernel, n_col),
        [f32(rows), f32(piece)] + [packed] * (INNER - 1),
        [where, offsets, taps, base, *others, *newer, *slots],
    )
    received = among_members(sends)
    [total] = call(total_kernel, [packed], [mine, *received])
    totals = [swapped(total, "lag", k * INNER) for k in range(1, n_outer)]
    older, *sends = call(
        functools.partial(prefix_kernel, n_outer),
        [f32(piece)] + [packed] * (INNER - 1),
        [where, mine, *received, *totals],
    )
    received = among_members(sends)
    [history_sum] = call(
        finish_kernel,
        [f32(rows)],
        [where, own, older, *received],
        [pltpu.VMEM((INNER, TICKS, piece, width), jnp.float32), pltpu.SemaphoreType.DMA((INNER,))],
        HBM,
    )
    return jnp.transpose(history_sum, (1, 0, 2))[None]


def solution(mesh):
    return jax.shard_map(
        local,
        mesh=mesh,
        in_specs=(P("lag", None, "col"), P("lag", "col", None), P("lag"), P("col", None)),
        out_specs=P("lag", "col", None, None),
        check_vma=False,
    )
```

```python
import functools

import jax
import jax.numpy as jnp
from jax import lax
from jax.experimental import pallas as pl
from jax.experimental.pallas import tpu as pltpu
from jax.sharding import PartitionSpec as P

TICKS = 3
PARTS = 2
INNER = 4
PADS = {2: 16, 3: 8}
MASKS = tuple(range(INNER - 1, 0, -1))
VMEM = pl.BlockSpec(memory_space=pltpu.VMEM)
SMEM = pl.BlockSpec(memory_space=pltpu.SMEM)
HBM = pl.BlockSpec(memory_space=pl.ANY)
LIMIT = pltpu.CompilerParams(vmem_limit_bytes=40 * 2**20)
FULL = pltpu.CompilerParams(vmem_limit_bytes=60 * 2**20)


def call(kernel, out_shape, ins, scratch=(), outs=VMEM, params=LIMIT):
    return pl.pallas_call(
        kernel,
        out_shape=out_shape,
        in_specs=[SMEM if a.ndim == 1 else VMEM for a in ins],
        out_specs=jax.tree.map(lambda _: outs, out_shape),
        scratch_shapes=list(scratch),
        compiler_params=params,
    )(*ins)


def swapped(value, axis, mask):
    count = lax.axis_size(axis)
    return lax.ppermute(value, axis, [(i, i ^ mask) for i in range(count)])


def pack(x, ref):
    ticks, half = x.shape[0], x.shape[1] // 2
    high = jnp.maximum(jnp.max(jnp.abs(x), axis=1, keepdims=True), 2.0**-100)
    power = jnp.floor(jnp.log2(high)) + 1.0
    q = jnp.clip(jnp.round(x * jnp.exp2(15.0 - power)), -32768.0, 32767.0).astype(jnp.int32)
    words = (q[:, :half] & 0xFFFF) | (q[:, half:] << 16)
    for t in range(ticks):
        ref[t * half : (t + 1) * half, :] = words[t]
    scales = power.astype(jnp.int32)
    tail = jnp.concatenate([scales[t] for t in range(ticks)] + [jnp.zeros((8 - ticks, x.shape[2]), jnp.int32)], axis=0)
    ref[ticks * half : ticks * half + 8, :] = tail


def unpack(ref, half):
    ticks = TICKS
    unit = jnp.exp2(ref[ticks * half : ticks * half + 8, :].astype(jnp.float32) - 15.0)
    values = []
    for t in range(ticks):
        words = ref[t * half : (t + 1) * half, :]
        both = jnp.concatenate([(words << 16) >> 16, words >> 16], axis=0)
        values.append(both.astype(jnp.float32) * unit[t : t + 1])
    return jnp.stack(values)


def chooser(slots):
    width = slots.shape[1]
    hit = lax.broadcasted_iota(jnp.int32, (width, width), 0) == slots[...]
    return hit.astype(jnp.float32).astype(jnp.bfloat16)


def prepare_kernel(where, offset, taps, own, slots, window, *sends):
    slots_own, _, width = own.shape
    chosen = chooser(slots)
    for t in range(TICKS):
        slot = offset[0] + t
        part = jnp.dot(own[jnp.minimum(slot, slots_own - 1)], chosen, preferred_element_type=jnp.float32)
        window[:, t * width : (t + 1) * width] = jnp.where(slot < slots_own, part, 0.0).astype(jnp.bfloat16)
    for k, out in enumerate(sends, 1):
        rows = out.shape[0]
        first = (where[0] ^ (1 + (k - 1) // PARTS)) * rows * PARTS + ((k - 1) % PARTS) * rows
        out[...] = taps[pl.ds(pl.multiple_of(first, rows), rows), :]


def ordered(newer, slots):
    chosen = chooser(slots)
    parts = [jnp.dot(newer[j], chosen, preferred_element_type=jnp.float32) for j in range(TICKS - 1)]
    return jnp.concatenate([part.astype(jnp.bfloat16) for part in parts], axis=1)


def used(where, offset, t, j):
    return (offset[0] + t == where[1] + j) & (where[2] == 0)


def base_kernel(n_col, where, offset, taps, newer, slots, *refs):
    cut = (n_col - 1) * PARTS
    others, windows, out = refs[:cut], refs[cut:-1], refs[-1]
    rows, width = out.shape[1:]
    late = ordered(newer, slots)
    ticks = []
    for t in range(TICKS):
        value = windows[0][:, t * width : (t + 1) * width]
        for j in range(t):
            value = jnp.where(used(where, offset, t, j), late[:, j * width : (j + 1) * width], value)
        ticks.append(value)
    right = jnp.concatenate(ticks, axis=1)
    part = rows // PARTS
    for p in range(PARTS):
        first = pl.multiple_of(where[0] * rows + p * part, part)
        total = jnp.dot(taps[pl.ds(first, part), :], right, preferred_element_type=jnp.float32)
        for i, window in enumerate(windows[1:]):
            total = total + jnp.dot(others[i * PARTS + p][...], window[...], preferred_element_type=jnp.float32)
        for t in range(TICKS):
            out[t, p * part : (p + 1) * part, :] = total[:, t * width : (t + 1) * width]


def late_kernel(n_col, where, offset, base, *refs):
    cut = (n_col - 1) * PARTS
    others, newer, slots = refs[:cut], refs[cut : cut + n_col - 1], refs[cut + n_col - 1 : cut + 2 * n_col - 2]
    own, mine, *sends = refs[cut + 2 * n_col - 2 :]
    _, rows, width = base.shape
    right = [ordered(*pair) for pair in zip(newer, slots)]
    part = rows // PARTS
    for p in range(PARTS):
        total = jnp.dot(others[p][...], right[0], preferred_element_type=jnp.float32)
        for i in range(1, n_col - 1):
            total = total + jnp.dot(others[i * PARTS + p][...], right[i], preferred_element_type=jnp.float32)
        for t in range(TICKS):
            value = base[t, p * part : (p + 1) * part, :]
            for j in range(t):
                value = value + jnp.where(used(where, offset, t, j), total[:, j * width : (j + 1) * width], 0.0)
            own[t, p * part : (p + 1) * part, :] = value
    piece = rows // INNER
    for k, out in zip((0, *MASKS), (mine, *sends)):
        first = pl.multiple_of((where[3] ^ k) * piece, piece)
        value = own[:, pl.ds(first, piece), :]
        if k:
            pack(value, out)
        else:
            out[...] = value


def total_kernel(mine, *refs):
    received, outs = refs[: INNER - 1], refs[INNER - 1 :]
    half = mine.shape[1] // 2
    total = mine[...]
    for ref in received:
        total = total + unpack(ref, half)
    size = TICKS * half + 8
    for i, out in enumerate(outs):
        if i:
            out[:size, :] = outs[0][:size, :]
        else:
            pack(total, out)
        if out.shape[0] > size:
            out[size:, :] = jnp.zeros((out.shape[0] - size, out.shape[1]), jnp.int32)


def inner_kernel(where, mine, *refs):
    received, outs = refs[: INNER - 1], refs[INNER - 1 :]
    half = mine.shape[1] // 2
    place = where[3]
    terms = [mine[...]] + [unpack(ref, half) for ref in received]
    for k, out in zip((0, *MASKS), outs):
        value = jnp.zeros(mine.shape, jnp.float32)
        for m, term in zip((0, *MASKS), terms):
            if m != k:
                value = value + jnp.where((place ^ m) < (place ^ k), term, 0.0)
        out[...] = value


def prefix_kernel(where, *refs):
    inner, totals, (base, *sends) = refs[:INNER], refs[INNER:-INNER], refs[-INNER:]
    half = base.shape[1] // 2
    group = where[4]
    earlier = jnp.zeros(base.shape, jnp.float32)
    for k, ref in enumerate(totals, 1):
        earlier = earlier + jnp.where((group ^ k) < group, unpack(ref, half), 0.0)
    base[...] = inner[0][...] + earlier
    for ref, out in zip(inner[1:], sends):
        pack(ref[...] + earlier, out)


def finish_kernel(where, own, base, *refs):
    received, (out, ready, sems) = refs[:-3], refs[-3:]
    piece = base.shape[1]
    copies = []
    for k, ref in zip((0, *MASKS), (base, *received)):
        first = pl.multiple_of((where[3] ^ k) * piece, piece)
        older = unpack(ref, piece // 2) if k else ref[...]
        ready[k] = own[:, pl.ds(first, piece), :] + older
        copies.append(pltpu.make_async_copy(ready.at[k], out.at[:, pl.ds(first, piece), :], sems.at[k]))
        copies[-1].start()
    for copy in copies:
        copy.wait()


def among_members(values):
    return [swapped(value, "lag", k) for k, value in zip(MASKS, values)]


def local(tap_matrices, density_history, offsets, column_slots):
    n_lag, n_col = lax.axis_size("lag"), lax.axis_size("col")
    n_outer = n_lag // INNER
    lag, col = lax.axis_index("lag"), lax.axis_index("col")
    slots_own, source, width = density_history.shape
    last = (lag == n_lag - 1).astype(jnp.int32)
    where = jnp.stack([col, jnp.int32(slots_own), last, lag & (INNER - 1), lag // INNER]).astype(jnp.int32)
    taps = tap_matrices[0]
    rows = taps.shape[0] // n_col
    piece = rows // INNER

    def f32(height):
        return jax.ShapeDtypeStruct((TICKS, height, width), jnp.float32)

    def bf16(*shape):
        return jax.ShapeDtypeStruct(shape, jnp.bfloat16)

    packed = jax.ShapeDtypeStruct((TICKS * piece // 2 + 8, width), jnp.int32)

    newer = lax.ppermute(density_history[: TICKS - 1], "lag", [(i, (i - 1) % n_lag) for i in range(n_lag)])
    window, *tap_sends = call(
        prepare_kernel,
        [bf16(source, TICKS * width)] + [bf16(rows // PARTS, source)] * ((n_col - 1) * PARTS),
        [where, offsets, taps, density_history, column_slots],
    )
    others = [swapped(value, "col", 1 + i // PARTS) for i, value in enumerate(tap_sends)]
    windows = [window] + [swapped(window, "col", k) for k in range(1, n_col)]
    [base] = call(
        functools.partial(base_kernel, n_col), [f32(rows)], [where, offsets, taps, newer, column_slots, *others, *windows]
    )
    newer = [swapped(newer, "col", k) for k in range(1, n_col)]
    slots = [swapped(column_slots, "col", k) for k in range(1, n_col)]
    own, mine, *sends = call(
        functools.partial(late_kernel, n_col),
        [f32(rows), f32(piece)] + [packed] * (INNER - 1),
        [where, offsets, base, *others, *newer, *slots],
    )
    received = among_members(sends)
    far = [jax.ShapeDtypeStruct((packed.shape[0] + PADS.get(k, 0), width), jnp.int32) for k in range(1, n_outer)]
    sums = call(total_kernel, far, [mine, *received])
    totals = [swapped(total, "lag", k * INNER) for k, total in enumerate(sums, 1)]
    inner = call(inner_kernel, [f32(piece)] * INNER, [where, mine, *received])
    older, *sends = call(prefix_kernel, [f32(piece)] + [packed] * (INNER - 1), [where, *inner, *totals])
    received = among_members(sends)
    [history_sum] = call(
        finish_kernel,
        [f32(rows)],
        [where, own, older, *received],
        [pltpu.VMEM((INNER, TICKS, piece, width), jnp.float32), pltpu.SemaphoreType.DMA((INNER,))],
        HBM,
    )
    return jnp.transpose(history_sum, (1, 0, 2))[None]


def solution(mesh):
    return jax.shard_map(
        local,
        mesh=mesh,
        in_specs=(P("lag", None, "col"), P("lag", "col", None), P("lag"), P("col", None)),
        out_specs=P("lag", "col", None, None),
        check_vma=False,
    )
```

```python
import functools

import jax
import jax.numpy as jnp
from jax import lax
from jax.experimental import pallas as pl
from jax.experimental.pallas import tpu as pltpu
from jax.sharding import PartitionSpec as P

TICKS = 3
PARTS = 2
INNER = 4
MASKS = tuple(range(INNER - 1, 0, -1))
VMEM = pl.BlockSpec(memory_space=pltpu.VMEM)
SMEM = pl.BlockSpec(memory_space=pltpu.SMEM)
HBM = pl.BlockSpec(memory_space=pl.ANY)
LIMIT = pltpu.CompilerParams(vmem_limit_bytes=40 * 2**20)
FULL = pltpu.CompilerParams(vmem_limit_bytes=60 * 2**20)


def call(kernel, out_shape, ins, scratch=(), outs=VMEM, params=LIMIT):
    return pl.pallas_call(
        kernel,
        out_shape=out_shape,
        in_specs=[SMEM if a.ndim == 1 else VMEM for a in ins],
        out_specs=jax.tree.map(lambda _: outs, out_shape),
        scratch_shapes=list(scratch),
        compiler_params=params,
    )(*ins)


def swapped(value, axis, mask):
    count = lax.axis_size(axis)
    return lax.ppermute(value, axis, [(i, i ^ mask) for i in range(count)])


def unit_of(eighths):
    return jnp.exp2(eighths * 0.125 - 15.0)


def pack(x, ref):
    ticks, half = x.shape[0], x.shape[1] // 2
    high = jnp.maximum(jnp.max(jnp.abs(x), axis=1, keepdims=True), 2.0**-100)
    eighths = jnp.floor(jnp.log2(high) * 8.0) + 1.0
    q = jnp.clip(jnp.round(x * (1.0 / unit_of(eighths))), -32768.0, 32767.0).astype(jnp.int32)
    words = (q[:, :half] & 0xFFFF) | (q[:, half:] << 16)
    for t in range(ticks):
        ref[t * half : (t + 1) * half, :] = words[t]
    scales = eighths.astype(jnp.int32)
    tail = jnp.concatenate([scales[t] for t in range(ticks)] + [jnp.zeros((8 - ticks, x.shape[2]), jnp.int32)], axis=0)
    ref[ticks * half : ticks * half + 8, :] = tail


def unpack(ref, half):
    ticks = TICKS
    unit = unit_of(ref[ticks * half : ticks * half + 8, :].astype(jnp.float32))
    values = []
    for t in range(ticks):
        words = ref[t * half : (t + 1) * half, :]
        both = jnp.concatenate([(words << 16) >> 16, words >> 16], axis=0)
        values.append(both.astype(jnp.float32) * unit[t : t + 1])
    return jnp.stack(values)


def chooser(slots):
    width = slots.shape[1]
    hit = lax.broadcasted_iota(jnp.int32, (width, width), 0) == slots[...]
    return hit.astype(jnp.float32).astype(jnp.bfloat16)


def prepare_kernel(where, offset, taps, own, slots, window, *sends):
    slots_own, _, width = own.shape
    chosen = chooser(slots)
    for t in range(TICKS):
        slot = offset[0] + t
        part = jnp.dot(own[jnp.minimum(slot, slots_own - 1)], chosen, preferred_element_type=jnp.float32)
        window[:, t * width : (t + 1) * width] = jnp.where(slot < slots_own, part, 0.0).astype(jnp.bfloat16)
    for k, out in enumerate(sends, 1):
        rows = out.shape[0]
        first = (where[0] ^ (1 + (k - 1) // PARTS)) * rows * PARTS + ((k - 1) % PARTS) * rows
        out[...] = taps[pl.ds(pl.multiple_of(first, rows), rows), :]


def ordered(newer, slots):
    chosen = chooser(slots)
    parts = [jnp.dot(newer[j], chosen, preferred_element_type=jnp.float32) for j in range(TICKS - 1)]
    return jnp.concatenate([part.astype(jnp.bfloat16) for part in parts], axis=1)


def used(where, offset, t, j):
    return (offset[0] + t == where[1] + j) & (where[2] == 0)


def base_kernel(n_col, where, offset, taps, newer, slots, *refs):
    cut = (n_col - 1) * PARTS
    others, windows, out = refs[:cut], refs[cut:-1], refs[-1]
    rows, width = out.shape[1:]
    late = ordered(newer, slots)
    ticks = []
    for t in range(TICKS):
        value = windows[0][:, t * width : (t + 1) * width]
        for j in range(t):
            value = jnp.where(used(where, offset, t, j), late[:, j * width : (j + 1) * width], value)
        ticks.append(value)
    right = jnp.concatenate(ticks, axis=1)
    part = rows // PARTS
    for p in range(PARTS):
        first = pl.multiple_of(where[0] * rows + p * part, part)
        total = jnp.dot(taps[pl.ds(first, part), :], right, preferred_element_type=jnp.float32)
        for i, window in enumerate(windows[1:]):
            total = total + jnp.dot(others[i * PARTS + p][...], window[...], preferred_element_type=jnp.float32)
        for t in range(TICKS):
            out[t, p * part : (p + 1) * part, :] = total[:, t * width : (t + 1) * width]


def late_kernel(n_col, where, offset, base, *refs):
    cut = (n_col - 1) * PARTS
    others, newer, slots = refs[:cut], refs[cut : cut + n_col - 1], refs[cut + n_col - 1 : cut + 2 * n_col - 2]
    own, mine, *sends = refs[cut + 2 * n_col - 2 :]
    _, rows, width = base.shape
    right = [ordered(*pair) for pair in zip(newer, slots)]
    part = rows // PARTS
    for p in range(PARTS):
        total = jnp.dot(others[p][...], right[0], preferred_element_type=jnp.float32)
        for i in range(1, n_col - 1):
            total = total + jnp.dot(others[i * PARTS + p][...], right[i], preferred_element_type=jnp.float32)
        for t in range(TICKS):
            value = base[t, p * part : (p + 1) * part, :]
            for j in range(t):
                value = value + jnp.where(used(where, offset, t, j), total[:, j * width : (j + 1) * width], 0.0)
            own[t, p * part : (p + 1) * part, :] = value
    piece = rows // INNER
    for k, out in zip((0, *MASKS), (mine, *sends)):
        first = pl.multiple_of((where[3] ^ k) * piece, piece)
        value = own[:, pl.ds(first, piece), :]
        if k:
            pack(value, out)
        else:
            out[...] = value


def total_kernel(mine, *refs):
    received, outs = refs[: INNER - 1], refs[INNER - 1 :]
    half = mine.shape[1] // 2
    total = mine[...]
    for ref in received:
        total = total + unpack(ref, half)
    pack(total, outs[0])
    for out in outs[1:]:
        out[...] = outs[0][...]


def inner_kernel(where, mine, *refs):
    received, outs = refs[: INNER - 1], refs[INNER - 1 :]
    half = mine.shape[1] // 2
    place = where[3]
    terms = [mine[...]] + [unpack(ref, half) for ref in received]
    for k, out in zip((0, *MASKS), outs):
        value = jnp.zeros(mine.shape, jnp.float32)
        for m, term in zip((0, *MASKS), terms):
            if m != k:
                value = value + jnp.where((place ^ m) < (place ^ k), term, 0.0)
        out[...] = value


def prefix_kernel(where, *refs):
    inner, totals, (base, *sends) = refs[:INNER], refs[INNER:-INNER], refs[-INNER:]
    half = base.shape[1] // 2
    group = where[4]
    earlier = jnp.zeros(base.shape, jnp.float32)
    for k, ref in enumerate(totals, 1):
        earlier = earlier + jnp.where((group ^ k) < group, unpack(ref, half), 0.0)
    base[...] = inner[0][...] + earlier
    for ref, out in zip(inner[1:], sends):
        pack(ref[...] + earlier, out)


def write_rows(where, own, pieces, out, ready, sems):
    copies = []
    for i, (k, older) in enumerate(pieces):
        piece = older.shape[1]
        first = pl.multiple_of((where[3] ^ k) * piece, piece)
        ready[i] = own[:, pl.ds(first, piece), :] + older
        copies.append(pltpu.make_async_copy(ready.at[i], out.at[:, pl.ds(first, piece), :], sems.at[i]))
        copies[-1].start()
    for copy in copies:
        copy.wait()


def own_rows_kernel(where, own, base, out, ready, sems):
    write_rows(where, own, [(0, base[...])], out, ready, sems)


def finish_kernel(where, own, *refs):
    received, out, ready, sems = refs[:-4], refs[-3], refs[-2], refs[-1]
    half = own.shape[1] // INNER // 2
    write_rows(where, own, ((k, unpack(ref, half)) for k, ref in zip(MASKS, received)), out, ready, sems)


def among_members(values):
    return [swapped(value, "lag", k) for k, value in zip(MASKS, values)]


def local(tap_matrices, density_history, offsets, column_slots):
    n_lag, n_col = lax.axis_size("lag"), lax.axis_size("col")
    n_outer = n_lag // INNER
    lag, col = lax.axis_index("lag"), lax.axis_index("col")
    slots_own, source, width = density_history.shape
    last = (lag == n_lag - 1).astype(jnp.int32)
    where = jnp.stack([col, jnp.int32(slots_own), last, lag & (INNER - 1), lag // INNER]).astype(jnp.int32)
    taps = tap_matrices[0]
    rows = taps.shape[0] // n_col
    piece = rows // INNER

    def f32(height):
        return jax.ShapeDtypeStruct((TICKS, height, width), jnp.float32)

    def bf16(*shape):
        return jax.ShapeDtypeStruct(shape, jnp.bfloat16)

    packed = jax.ShapeDtypeStruct((TICKS * piece // 2 + 8, width), jnp.int32)

    newer = lax.ppermute(density_history[: TICKS - 1], "lag", [(i, (i - 1) % n_lag) for i in range(n_lag)])
    window, *tap_sends = call(
        prepare_kernel,
        [bf16(source, TICKS * width)] + [bf16(rows // PARTS, source)] * ((n_col - 1) * PARTS),
        [where, offsets, taps, density_history, column_slots],
    )
    others = [swapped(value, "col", 1 + i // PARTS) for i, value in enumerate(tap_sends)]
    windows = [window] + [swapped(window, "col", k) for k in range(1, n_col)]
    [base] = call(
        functools.partial(base_kernel, n_col), [f32(rows)], [where, offsets, taps, newer, column_slots, *others, *windows]
    )
    newer = [swapped(newer, "col", k) for k in range(1, n_col)]
    slots = [swapped(column_slots, "col", k) for k in range(1, n_col)]
    own, mine, *sends = call(
        functools.partial(late_kernel, n_col),
        [f32(rows), f32(piece)] + [packed] * (INNER - 1),
        [where, offsets, base, *others, *newer, *slots],
    )
    received = among_members(sends)
    sums = call(total_kernel, [packed] * (n_outer - 1), [mine, *received])
    totals = [swapped(total, "lag", k * INNER) for k, total in enumerate(sums, 1)]
    inner = call(inner_kernel, [f32(piece)] * INNER, [where, mine, *received])
    older, *sends = call(prefix_kernel, [f32(piece)] + [packed] * (INNER - 1), [where, *inner, *totals])
    received = among_members(sends)
    [history_sum] = call(
        own_rows_kernel,
        [f32(rows)],
        [where, own, older],
        [pltpu.VMEM((1, TICKS, piece, width), jnp.float32), pltpu.SemaphoreType.DMA((1,))],
        HBM,
    )
    history_sum = pl.pallas_call(
        finish_kernel,
        out_shape=f32(rows),
        in_specs=[SMEM] + [VMEM] * INNER + [HBM],
        out_specs=HBM,
        scratch_shapes=[
            pltpu.VMEM((INNER - 1, TICKS, piece, width), jnp.float32),
            pltpu.SemaphoreType.DMA((INNER - 1,)),
        ],
        input_output_aliases={INNER + 1: 0},
        compiler_params=LIMIT,
    )(where, own, *received, history_sum)
    return jnp.transpose(history_sum, (1, 0, 2))[None]


def solution(mesh):
    return jax.shard_map(
        local,
        mesh=mesh,
        in_specs=(P("lag", None, "col"), P("lag", "col", None), P("lag"), P("col", None)),
        out_specs=P("lag", "col", None, None),
        check_vma=False,
    )
```

```python
import functools

import jax
import jax.numpy as jnp
from jax import lax
from jax.experimental import pallas as pl
from jax.experimental.pallas import tpu as pltpu
from jax.sharding import PartitionSpec as P

TICKS = 3
PARTS = 2
INNER = 4
MASKS = tuple(range(INNER - 1, 0, -1))
VMEM = pl.BlockSpec(memory_space=pltpu.VMEM)
SMEM = pl.BlockSpec(memory_space=pltpu.SMEM)
HBM = pl.BlockSpec(memory_space=pl.ANY)
LIMIT = pltpu.CompilerParams(vmem_limit_bytes=40 * 2**20)
FULL = pltpu.CompilerParams(vmem_limit_bytes=60 * 2**20)


def call(kernel, out_shape, ins, scratch=(), outs=VMEM, params=LIMIT):
    return pl.pallas_call(
        kernel,
        out_shape=out_shape,
        in_specs=[SMEM if a.ndim == 1 else VMEM for a in ins],
        out_specs=jax.tree.map(lambda _: outs, out_shape),
        scratch_shapes=list(scratch),
        compiler_params=params,
    )(*ins)


def swapped(value, axis, mask):
    count = lax.axis_size(axis)
    return lax.ppermute(value, axis, [(i, i ^ mask) for i in range(count)])


def unit_of(eighths):
    return jnp.exp2(eighths * 0.125 - 15.0)


def pack(x, ref):
    ticks, half = x.shape[0], x.shape[1] // 2
    high = jnp.maximum(jnp.max(jnp.abs(x), axis=1, keepdims=True), 2.0**-100)
    eighths = jnp.floor(jnp.log2(high) * 8.0) + 1.0
    q = jnp.clip(jnp.round(x * (1.0 / unit_of(eighths))), -32768.0, 32767.0).astype(jnp.int32)
    words = (q[:, :half] & 0xFFFF) | (q[:, half:] << 16)
    for t in range(ticks):
        ref[t * half : (t + 1) * half, :] = words[t]
    scales = eighths.astype(jnp.int32)
    tail = jnp.concatenate([scales[t] for t in range(ticks)] + [jnp.zeros((8 - ticks, x.shape[2]), jnp.int32)], axis=0)
    ref[ticks * half : ticks * half + 8, :] = tail


def unpack(ref, half):
    ticks = TICKS
    unit = unit_of(ref[ticks * half : ticks * half + 8, :].astype(jnp.float32))
    values = []
    for t in range(ticks):
        words = ref[t * half : (t + 1) * half, :]
        both = jnp.concatenate([(words << 16) >> 16, words >> 16], axis=0)
        values.append(both.astype(jnp.float32) * unit[t : t + 1])
    return jnp.stack(values)


def chooser(slots):
    width = slots.shape[1]
    hit = lax.broadcasted_iota(jnp.int32, (width, width), 0) == slots[...]
    return hit.astype(jnp.float32).astype(jnp.bfloat16)


def prepare_kernel(where, offset, taps, own, slots, window, *sends):
    slots_own, _, width = own.shape
    chosen = chooser(slots)
    for t in range(TICKS):
        slot = offset[0] + t
        part = jnp.dot(own[jnp.minimum(slot, slots_own - 1)], chosen, preferred_element_type=jnp.float32)
        window[:, t * width : (t + 1) * width] = jnp.where(slot < slots_own, part, 0.0).astype(jnp.bfloat16)
    for k, out in enumerate(sends, 1):
        rows = out.shape[0]
        first = (where[0] ^ (1 + (k - 1) // PARTS)) * rows * PARTS + ((k - 1) % PARTS) * rows
        out[...] = taps[pl.ds(pl.multiple_of(first, rows), rows), :]


def ordered(newer, slots):
    chosen = chooser(slots)
    parts = [jnp.dot(newer[j], chosen, preferred_element_type=jnp.float32) for j in range(TICKS - 1)]
    return jnp.concatenate([part.astype(jnp.bfloat16) for part in parts], axis=1)


def used(where, offset, t, j):
    return (offset[0] + t == where[1] + j) & (where[2] == 0)


def base_kernel(n_col, where, offset, taps, newer, slots, *refs):
    cut = (n_col - 1) * PARTS
    others, windows, out = refs[:cut], refs[cut:-1], refs[-1]
    rows, width = out.shape[1:]
    late = ordered(newer, slots)
    ticks = []
    for t in range(TICKS):
        value = windows[0][:, t * width : (t + 1) * width]
        for j in range(t):
            value = jnp.where(used(where, offset, t, j), late[:, j * width : (j + 1) * width], value)
        ticks.append(value)
    right = jnp.concatenate(ticks, axis=1)
    part = rows // PARTS
    for p in range(PARTS):
        first = pl.multiple_of(where[0] * rows + p * part, part)
        total = jnp.dot(taps[pl.ds(first, part), :], right, preferred_element_type=jnp.float32)
        for i, window in enumerate(windows[1:]):
            total = total + jnp.dot(others[i * PARTS + p][...], window[...], preferred_element_type=jnp.float32)
        for t in range(TICKS):
            out[t, p * part : (p + 1) * part, :] = total[:, t * width : (t + 1) * width]


def late_kernel(n_col, where, offset, base, *refs):
    cut = (n_col - 1) * PARTS
    others, newer, slots = refs[:cut], refs[cut : cut + n_col - 1], refs[cut + n_col - 1 : cut + 2 * n_col - 2]
    own, mine, *sends = refs[cut + 2 * n_col - 2 :]
    _, rows, width = base.shape
    right = [ordered(*pair) for pair in zip(newer, slots)]
    part = rows // PARTS
    for p in range(PARTS):
        total = jnp.dot(others[p][...], right[0], preferred_element_type=jnp.float32)
        for i in range(1, n_col - 1):
            total = total + jnp.dot(others[i * PARTS + p][...], right[i], preferred_element_type=jnp.float32)
        for t in range(TICKS):
            value = base[t, p * part : (p + 1) * part, :]
            for j in range(t):
                value = value + jnp.where(used(where, offset, t, j), total[:, j * width : (j + 1) * width], 0.0)
            own[t, p * part : (p + 1) * part, :] = value
    piece = rows // INNER
    for k, out in zip((0, *MASKS), (mine, *sends)):
        first = pl.multiple_of((where[3] ^ k) * piece, piece)
        value = own[:, pl.ds(first, piece), :]
        if k:
            pack(value, out)
        else:
            out[...] = value


def total_kernel(mine, *refs):
    received, outs = refs[: INNER - 1], refs[INNER - 1 :]
    half = mine.shape[1] // 2
    total = mine[...]
    for ref in received:
        total = total + unpack(ref, half)
    pack(total, outs[0])
    for out in outs[1:]:
        out[...] = outs[0][...]


def inner_kernel(where, mine, *refs):
    received, outs = refs[: INNER - 1], refs[INNER - 1 :]
    half = mine.shape[1] // 2
    place = where[3]
    terms = [mine[...]] + [unpack(ref, half) for ref in received]
    for k, out in zip((0, *MASKS), outs):
        value = jnp.zeros(mine.shape, jnp.float32)
        for m, term in zip((0, *MASKS), terms):
            if m != k:
                value = value + jnp.where((place ^ m) < (place ^ k), term, 0.0)
        out[...] = value


def prefix_kernel(where, *refs):
    inner, totals, (base, *sends) = refs[:INNER], refs[INNER:-INNER], refs[-INNER:]
    half = base.shape[1] // 2
    group = where[4]
    earlier = jnp.zeros(base.shape, jnp.float32)
    for k, ref in zip(range(len(totals), 0, -1), totals):
        earlier = earlier + jnp.where(group >= k, unpack(ref, half), 0.0)
    base[...] = inner[0][...] + earlier
    for ref, out in zip(inner[1:], sends):
        pack(ref[...] + earlier, out)


def write_rows(where, own, pieces, out, ready, sems):
    copies = []
    for i, (k, older) in enumerate(pieces):
        piece = older.shape[1]
        first = pl.multiple_of((where[3] ^ k) * piece, piece)
        ready[i] = own[:, pl.ds(first, piece), :] + older
        copies.append(pltpu.make_async_copy(ready.at[i], out.at[:, pl.ds(first, piece), :], sems.at[i]))
        copies[-1].start()
    for copy in copies:
        copy.wait()


def own_rows_kernel(where, own, base, out, ready, sems):
    write_rows(where, own, [(0, base[...])], out, ready, sems)


def finish_kernel(where, own, *refs):
    received, out, ready, sems = refs[:-4], refs[-3], refs[-2], refs[-1]
    half = own.shape[1] // INNER // 2
    write_rows(where, own, ((k, unpack(ref, half)) for k, ref in zip(MASKS, received)), out, ready, sems)


def among_members(values):
    return [swapped(value, "lag", k) for k, value in zip(MASKS, values)]


def local(tap_matrices, density_history, offsets, column_slots):
    n_lag, n_col = lax.axis_size("lag"), lax.axis_size("col")
    n_outer = n_lag // INNER
    lag, col = lax.axis_index("lag"), lax.axis_index("col")
    slots_own, source, width = density_history.shape
    last = (lag == n_lag - 1).astype(jnp.int32)
    where = jnp.stack([col, jnp.int32(slots_own), last, lag & (INNER - 1), lag // INNER]).astype(jnp.int32)
    taps = tap_matrices[0]
    rows = taps.shape[0] // n_col
    piece = rows // INNER

    def f32(height):
        return jax.ShapeDtypeStruct((TICKS, height, width), jnp.float32)

    def bf16(*shape):
        return jax.ShapeDtypeStruct(shape, jnp.bfloat16)

    packed = jax.ShapeDtypeStruct((TICKS * piece // 2 + 8, width), jnp.int32)

    newer = lax.ppermute(density_history[: TICKS - 1], "lag", [(i, (i - 1) % n_lag) for i in range(n_lag)])
    window, *tap_sends = call(
        prepare_kernel,
        [bf16(source, TICKS * width)] + [bf16(rows // PARTS, source)] * ((n_col - 1) * PARTS),
        [where, offsets, taps, density_history, column_slots],
    )
    others = [swapped(value, "col", 1 + i // PARTS) for i, value in enumerate(tap_sends)]
    windows = [window] + [swapped(window, "col", k) for k in range(1, n_col)]
    [base] = call(
        functools.partial(base_kernel, n_col), [f32(rows)], [where, offsets, taps, newer, column_slots, *others, *windows]
    )
    newer = [swapped(newer, "col", k) for k in range(1, n_col)]
    slots = [swapped(column_slots, "col", k) for k in range(1, n_col)]
    own, mine, *sends = call(
        functools.partial(late_kernel, n_col),
        [f32(rows), f32(piece)] + [packed] * (INNER - 1),
        [where, offsets, base, *others, *newer, *slots],
    )
    received = among_members(sends)
    sums = call(total_kernel, [packed] * (n_outer - 1), [mine, *received])
    totals = [
        lax.ppermute(total, "lag", [(i, (i + k * INNER) % n_lag) for i in range(n_lag)]) for k, total in zip(range(n_outer - 1, 0, -1), sums)
    ]
    inner = call(inner_kernel, [f32(piece)] * INNER, [where, mine, *received])
    older, *sends = call(prefix_kernel, [f32(piece)] + [packed] * (INNER - 1), [where, *inner, *totals])
    received = among_members(sends)
    [history_sum] = call(
        own_rows_kernel,
        [f32(rows)],
        [where, own, older],
        [pltpu.VMEM((1, TICKS, piece, width), jnp.float32), pltpu.SemaphoreType.DMA((1,))],
        HBM,
    )
    history_sum = pl.pallas_call(
        finish_kernel,
        out_shape=f32(rows),
        in_specs=[SMEM] + [VMEM] * INNER + [HBM],
        out_specs=HBM,
        scratch_shapes=[
            pltpu.VMEM((INNER - 1, TICKS, piece, width), jnp.float32),
            pltpu.SemaphoreType.DMA((INNER - 1,)),
        ],
        input_output_aliases={INNER + 1: 0},
        compiler_params=LIMIT,
    )(where, own, *received, history_sum)
    return jnp.transpose(history_sum, (1, 0, 2))[None]


def solution(mesh):
    return jax.shard_map(
        local,
        mesh=mesh,
        in_specs=(P("lag", None, "col"), P("lag", "col", None), P("lag"), P("col", None)),
        out_specs=P("lag", "col", None, None),
        check_vma=False,
    )
```
